32 devices in a mesh: rep: 2 (over x), dp: 8 (over z, y), tensor: 2 (over core).
Axes of the slice: x: 2, y: 2, z: 4, core: 2. Of those that a mesh axis runs over, the one named last changes fastest.
Arguments:
- normed_hidden_state: bfloat16 [1024, 8192], P(('rep', 'dp'), 'tensor'), parts along dimension 0, may hold values from -6 to 6
- queries: bfloat16 [1024, 2, 4096], P(('rep', 'dp'), None, 'tensor'), parts along dimension 0
- key_value_cache: bfloat16 [1024, 2, 128, 512], P(('rep', 'dp'), None, None, 'tensor'), parts along dimension 0
- base_projection_weight: bfloat16 [8192, 2, 512], P('tensor'), may hold values from -0.0625 to 0.0625
- adapter_down_weight: bfloat16 [8, 8192, 128], P('dp', 'tensor'), may hold values from -0.0625 to 0.0625
- adapter_up_weight: bfloat16 [8, 2, 64, 512], P('dp', None, None, 'tensor'), may hold values from -0.75 to 0.75
- adapter_index_rows: int32 [1024, 1], P(('rep', 'dp')), parts along dimension 0, may hold values from 0 to 7; in each aligned block of 64 rows (0 to 63, 64 to 127, ...) at most 16 rows name the same one
- placement: int32 [8], replicated, may hold values from 0 to 7, each once
- lengths: int32 [1024], P(('rep', 'dp')), parts along dimension 0, may hold values from 2 to 128, as said below
Outputs:
- attention_out: bfloat16 [1024, 2, 4096], P(('rep', 'dp'), None, 'tensor'), parts along dimension 0
- new_kv: bfloat16 [1024, 2, 512], P(('rep', 'dp'), None, 'tensor'), parts along dimension 0
The draws below stay inside these ranges and needn't reach their ends.
There are 2 independent parts, one for each index of `rep`. The reference program is written for one: setup_inputs(seed, part) draws one part's arguments, and reference() takes and returns one part's arrays. A program takes and returns all parts, laid end to end along the dimension named above; an argument that names none is the same for every part. Nothing has to cross between parts.
Inputs may be any that keep to these rules, and one draw needn't show every extreme that they name: `adapter_index_rows`: in the rows of one index of dp, no adapter is named by more than 16 rows, a bound that some block reaches. `placement`: each adapter has one slot. `lengths`: every 16th row has all 128 slots filled.
All inputs are finite; a program needn't handle non-finite values.
Results may differ from the reference program's by a relative error of at most 0.0054.
Values may be sent and summed in bfloat16 or wider, within the bound.
A program may use at most 128 MiB of HBM per device.

```python
import math
import jax
import jax.numpy as jnp
import numpy as np
from jax import lax

MODEL_WIDTH = 8192
QH = 32
KEY_VALUE_HEADS = 4
HEAD_SIZE = 128
ADAPTER_RANK = 64
ROW_DEV = 64
CTX = 128
ROWS = 512
ADAPTER_COUNT = 8
CAP = 16


def cache_noise(key):
    return jax.random.normal(key, (ROWS, 2, CTX, KEY_VALUE_HEADS * HEAD_SIZE), jnp.float32)


def draw_key_value_cache(key, part):
    noise = cache_noise(key)
    return noise.astype(jnp.bfloat16)


def draw_queries(key, part):
    key = jax.random.fold_in(key, 12)
    fresh = jax.random.normal(key, (ROWS, 2, QH * HEAD_SIZE), jnp.float32)
    return fresh.astype(jnp.bfloat16)


def draw_lengths(key, part):
    key = jax.random.fold_in(key, 13)
    drawn = jax.random.randint(key, (ROWS,), 2, CTX + 1)
    return jnp.where(jnp.arange(ROWS) % 16 == 0, CTX, drawn).astype(jnp.int32)


def block_scale(stream_key, shape, cuts, smallest, top_value):
    factor_of, own = 1.0, jax.random.fold_in(stream_key, 6)
    for position, blocks in cuts:
        steps = jnp.exp(jax.random.uniform(jax.random.fold_in(own, position), (blocks,), jnp.float32, smallest / len(cuts), top_value / len(cuts)))
        factor_of = factor_of * jnp.repeat(steps, shape[position] // blocks).reshape([-1 if axis == position else 1 for axis in range(len(shape))])
    return factor_of


def shared_out(key, own, number, rows, amount, top, most, slope):
    order = jax.random.permutation(key, amount)
    crowded, usual = load_shares(amount, rows * top, most, slope, True), load_shares(amount, rows * top, most, slope, False)
    places = jnp.arange(amount)

    def named(sizes, offset_by):
        used = int((sizes > 0).sum())
        fixed = max(1, used // 4)
        passed = fixed + (places - fixed + offset_by * (used - fixed)) % max(1, amount - fixed)
        return jnp.zeros((amount,), jnp.int32).at[order[jnp.where(places < fixed, places, passed)]].set(jnp.asarray(sizes, jnp.int32))

    sizes = jnp.where(number % 4 == 0, named(crowded, number // 4), named(usual, number - number // 4 - 1))
    mixed = jax.random.permutation(jax.random.fold_in(own, 3), amount)
    source_of, sink = mixed[0:amount // 2 * 2:2], mixed[1:amount // 2 * 2:2]
    room = jnp.minimum(sizes[source_of] - 1, most - sizes[sink]) // 2
    room = jnp.where((source_of == order[0]) | (sink == order[0]) | (sizes[sink] == 0), 0, jnp.maximum(room, 0))
    passed = jax.random.randint(jax.random.fold_in(own, 4), (amount // 2,), 0, 1 << 20) % (room + 1)
    sizes = sizes.at[source_of].add(-passed).at[sink].add(passed)
    items = jnp.searchsorted(jnp.cumsum(sizes), jnp.arange(rows * top), side="right").astype(jnp.int32)
    listing = items.reshape(top, rows).T
    listing = listing[jax.random.permutation(jax.random.fold_in(own, 1), rows)]
    offset_by = jax.random.randint(jax.random.fold_in(own, 2), (rows, 1), 0, top)
    return jnp.take_along_axis(listing, (jnp.arange(top)[None, :] + offset_by) % top, axis=1)


def load_shares(amount, total, bound, lean, full):
    portions = [(1 << 20) // math.isqrt(standing ** lean) + 1 for standing in range(1, amount + 1)]
    largest = bound if full else min(bound, max(-(-total // amount), total * portions[0] // sum(portions)))
    least = 1 if total - largest >= amount - 1 else 0
    holding, spare = [largest] + [least] * (amount - 1), total - largest - least * (amount - 1)
    while spare > 0:
        candidates = [i for i in range(1, amount) if holding[i] < largest] or [i for i in range(1, amount) if holding[i] < bound]
        whole, budget = sum([portions[i] for i in candidates]), spare
        for i in candidates:
            more = min(bound - holding[i], max(1, budget * portions[i] // whole), spare)
            holding[i] = holding[i] + more
            spare = spare - more
    return np.array(holding)


def centred(own_key, dims, scale, bound, shards=(), held_as=jnp.bfloat16):
    values = jax.random.normal(own_key, dims, jnp.float32) * scale
    if len(shards) > 0:
        values = block_scale(own_key, dims, shards, -0.22, 0.18) * values
    return jnp.clip(values, min=-bound, max=bound).astype(held_as)


def setup_inputs(seed: int = 0, part: int = 0) -> dict:
    key_of = jax.random.split(jax.random.key(seed), 10)
    own_keys = jax.random.split(jax.random.fold_in(key_of[9], part), 10)
    normed_hidden_state = centred(own_keys[0], (ROWS, MODEL_WIDTH), 1.0, 6.0, ((0, 8), (1, 2)))
    queries = draw_queries(jax.random.fold_in(jax.random.fold_in(key_of[9], part), 71), part)
    key_value_cache = draw_key_value_cache(jax.random.fold_in(jax.random.fold_in(key_of[9], part), 71), part)
    base_projection_weight = centred(key_of[3], (MODEL_WIDTH, 2, KEY_VALUE_HEADS * HEAD_SIZE), MODEL_WIDTH ** -0.5, 0.0625, ((0, 2),))
    adapter_down_weight = centred(key_of[4], (ADAPTER_COUNT, MODEL_WIDTH, 2 * ADAPTER_RANK), MODEL_WIDTH ** -0.5, 0.0625, ((0, 8), (1, 2)))
    adapter_up_weight = centred(key_of[5], (ADAPTER_COUNT, 2, ADAPTER_RANK, KEY_VALUE_HEADS * HEAD_SIZE), ADAPTER_RANK ** -0.5, 0.75, ((0, 8), (3, 2)))
    adapter_index_rows_keys = jax.random.split(jax.random.fold_in(own_keys[6], 1), ROWS // ROW_DEV)
    adapter_index_rows_turns = jax.random.permutation(jax.random.fold_in(own_keys[6], 3), ROWS // ROW_DEV)
    adapter_index_rows = jax.vmap(lambda own, number: shared_out(jax.random.fold_in(own_keys[6], 2), own, number, ROW_DEV, ADAPTER_COUNT, 1, CAP, 2))(adapter_index_rows_keys, adapter_index_rows_turns).reshape((ROWS, 1))
    placement = jax.random.permutation(key_of[7], ADAPTER_COUNT).astype(jnp.int32)
    lengths = draw_lengths(jax.random.fold_in(jax.random.fold_in(key_of[9], part), 71), part)
    return dict(normed_hidden_state=normed_hidden_state, queries=queries, key_value_cache=key_value_cache, base_projection_weight=base_projection_weight, adapter_down_weight=adapter_down_weight, adapter_up_weight=adapter_up_weight, adapter_index_rows=adapter_index_rows, placement=placement, lengths=lengths)


def attend(queries, key_value_cache, new_kv, lengths):
    rows = queries.shape[0]
    groups = key_value_cache.shape[3] // HEAD_SIZE
    per_group = queries.shape[2] // (HEAD_SIZE * groups)
    query = queries.astype(jnp.float32).reshape(rows, 2, groups, per_group, HEAD_SIZE)
    keys = key_value_cache[:, 0].astype(jnp.float32).reshape(rows, -1, groups, HEAD_SIZE)
    values = key_value_cache[:, 1].astype(jnp.float32).reshape(rows, -1, groups, HEAD_SIZE)
    new_key = new_kv[:, 0, :].astype(jnp.float32).reshape(rows, groups, HEAD_SIZE)
    new_value = new_kv[:, 1, :].astype(jnp.float32).reshape(rows, groups, HEAD_SIZE)
    scale = HEAD_SIZE ** -0.5
    old_scores = jnp.einsum("rlgqh,rpgh->rlgqp", query, keys, precision=lax.Precision.HIGHEST) * scale
    positions = jnp.arange(key_value_cache.shape[2], dtype=jnp.int32)
    valid = positions[None, :] < lengths[:, None]
    old_scores = jnp.where(valid[:, None, None, None, :], old_scores, -1e30)
    new_scores = jnp.einsum("rlgqh,rgh->rlgq", query, new_key, precision=lax.Precision.HIGHEST) * scale
    top = jnp.maximum(jnp.max(old_scores, axis=-1), new_scores)
    old_weights = jnp.exp(old_scores - top[..., None])
    new_weights = jnp.exp(new_scores - top)
    total = jnp.sum(old_weights, axis=-1) + new_weights
    old_probs = (old_weights / total[..., None]).astype(jnp.bfloat16).astype(jnp.float32)
    new_probs = (new_weights / total).astype(jnp.bfloat16).astype(jnp.float32)
    mixed = jnp.einsum("rlgqp,rpgh->rlgqh", old_probs, values, precision=lax.Precision.HIGHEST)
    mixed = mixed + new_probs[..., None] * new_value[:, None, :, None, :]
    return mixed.astype(jnp.bfloat16).reshape(rows, 2, -1)


def reference(normed_hidden_state, queries, key_value_cache, base_projection_weight, adapter_down_weight, adapter_up_weight, adapter_index_rows, placement, lengths):
    slots = placement[adapter_index_rows[:, 0]]
    rows = normed_hidden_state.shape[0]
    base = jnp.dot(normed_hidden_state, base_projection_weight.reshape(base_projection_weight.shape[0], -1), preferred_element_type=jnp.float32).reshape(rows, 2, -1)

    def add_middle(total, slot_index):
        mask = (slots == slot_index).astype(jnp.float32)
        adapter_term = jnp.dot(normed_hidden_state, adapter_down_weight[slot_index], preferred_element_type=jnp.float32)
        return total + mask[:, None] * adapter_term, None

    middle, _ = lax.scan(add_middle, jnp.zeros((rows, 2 * ADAPTER_RANK), jnp.float32), jnp.arange(ADAPTER_COUNT, dtype=jnp.int32))
    layer_pair = middle.reshape(rows, 2, ADAPTER_RANK)

    def add_delta(total, slot_index):
        mask = (slots == slot_index).astype(jnp.float32)
        adapter_term = jnp.einsum("ail,ilt->ait", layer_pair, adapter_up_weight[slot_index].astype(jnp.float32), precision=lax.Precision.HIGHEST)
        return total + mask[:, None, None] * adapter_term, None

    delta, _ = lax.scan(add_delta, jnp.zeros(base.shape, jnp.float32), jnp.arange(ADAPTER_COUNT, dtype=jnp.int32))
    new_kv = (base + delta).astype(jnp.bfloat16)
    return attend(queries, key_value_cache, new_kv, lengths), new_kv
```

```python
import functools

import jax
import jax.numpy as jnp
from jax import lax
from jax.experimental import pallas as pl
from jax.experimental.pallas import tpu as pltpu
from jax.sharding import PartitionSpec as P

HEAD = 128
MESH = pl.DeviceIdType.MESH
BF16 = jnp.bfloat16
F32 = jnp.float32
SLOTS = 16


def iota(shape, dim):
    return lax.broadcasted_iota(jnp.int32, shape, dim)


def kernel(
    n,
    hid_ref,
    idx_ref,
    place_ref,
    len_ref,
    up_ref,
    q_hbm,
    cache_hbm,
    w_hbm,
    d_hbm,
    out_ref,
    kv_ref,
    qbuf,
    cbuf,
    wbuf,
    dbuf,
    sendbuf,
    recvbuf,
    wide,
    back_t,
    base,
    base_in,
    mid,
    mid_in,
    ans,
    ret,
    newkv,
    top,
    total,
    mixed,
    local_sem,
    w_sem,
    out_send,
    out_recv,
    ret_send,
    ret_recv,
    pair_send,
    pair_recv,
):
    rows, width = hid_ref.shape
    tiles = wbuf.shape[0]
    half = tiles // 2
    groups = cbuf.shape[3] // HEAD
    slots = n * SLOTS
    me = lax.axis_index("dp")
    side = lax.axis_index("tensor")
    other = 1 - side
    per_row = qbuf.shape[0] // rows
    per_group = per_row // groups

    loads = [
        pltpu.make_async_copy(q_hbm, qbuf, local_sem.at[0]),
        pltpu.make_async_copy(cache_hbm, cbuf, local_sem.at[1]),
        pltpu.make_async_copy(d_hbm, dbuf, local_sem.at[2]),
    ]
    w_loads = [
        pltpu.make_async_copy(w_hbm.at[:, :, pl.ds(c * 128, 128)], wbuf.at[c], w_sem.at[c])
        for c in range(tiles)
    ]

    barrier = pltpu.get_barrier_semaphore()
    for o in range(1, n):
        pl.semaphore_signal(
            barrier, inc=1, device_id={"dp": lax.rem(me + o, n)}, device_id_type=MESH
        )
    pl.semaphore_signal(barrier, inc=1, device_id={"tensor": other}, device_id_type=MESH)
    for copy in w_loads:
        copy.start()
    for copy in loads:
        copy.start()

    index = idx_ref[...]
    slot = jnp.zeros((1, rows), jnp.int32)
    for a in range(n):
        slot = slot + jnp.where(index == a, place_ref[a], 0)
    slot = slot.astype(F32)
    first, second = iota((rows, rows), 0), iota((rows, rows), 1)
    across = jnp.broadcast_to(slot, (rows, rows))
    down = jnp.sum(jnp.where(first == second, across, 0.0), axis=1, keepdims=True)
    same = jnp.where((down == across) & (first < second), 1.0, 0.0)
    target = slot * SLOTS + jnp.sum(same, axis=0, keepdims=True)
    target_down = jnp.sum(
        jnp.where(first == second, jnp.broadcast_to(target, (rows, rows)), 0.0),
        axis=1,
        keepdims=True,
    )
    placing = jnp.where(iota((slots, rows), 0).astype(F32) == target, 1.0, 0.0).astype(BF16)
    back_t[...] = jnp.where(
        iota((rows, slots), 1).astype(F32) == target_down, 1.0, 0.0
    ).astype(BF16)
    step = 1024
    for c in range(0, width, step):
        sendbuf[:, c : c + step] = jnp.dot(
            placing, hid_ref[:, c : c + step], preferred_element_type=F32
        ).astype(BF16)

    pl.semaphore_wait(barrier, n)
    mine = pl.ds(pl.multiple_of(me * SLOTS, SLOTS), SLOTS)

    def block(d):
        return pl.ds(pl.multiple_of(d * SLOTS, SLOTS), SLOTS)

    order = sorted(range(1, n), key=lambda o: -min(o, n - o))
    dispatch = []
    for o in order:
        d = lax.rem(me + o, n)
        dispatch.append(
            pltpu.make_async_remote_copy(
                src_ref=sendbuf.at[block(d), :],
                dst_ref=recvbuf.at[mine, :],
                send_sem=out_send.at[o],
                recv_sem=out_recv.at[o],
                device_id={"dp": d},
                device_id_type=MESH,
            )
        )
    for copy in dispatch:
        copy.start()
    recvbuf[mine, :] = sendbuf[mine, :]

    deep = 256
    spreads = [
        jnp.where(iota((deep, 2 * deep), 1) == 2 * iota((deep, 2 * deep), 0) + j, 1.0, 0.0).astype(
            BF16
        )
        for j in range(2)
    ]
    gang = 4
    for c in range(0, width, gang * deep):
        stack = jnp.concatenate(
            [hid_ref[:, c + i * deep : c + (i + 1) * deep] for i in range(gang)], axis=0
        )
        for j in range(2):
            res = jnp.dot(stack, spreads[j], preferred_element_type=F32).astype(BF16)
            for i in range(gang):
                at = 2 * (c + i * deep)
                wide[j * rows : (j + 1) * rows, at : at + 2 * deep] = res[
                    i * rows : (i + 1) * rows
                ]
    for copy in w_loads:
        copy.wait()
    chunk = 2048
    for h in range(2):
        acc = jnp.zeros((2 * rows, half * 128), F32)
        for k in range(0, 2 * width, chunk):
            rhs = jnp.concatenate(
                [
                    wbuf.at[h * half + c].reshape(2 * width, 128)[k : k + chunk, :]
                    for c in range(half)
                ],
                axis=1,
            )
            acc = acc + jnp.dot(wide[:, k : k + chunk], rhs, preferred_element_type=F32)
        base[h] = acc
    base_copy = pltpu.make_async_remote_copy(
        src_ref=base.at[other],
        dst_ref=base_in,
        send_sem=pair_send.at[0],
        recv_sem=pair_recv.at[0],
        device_id={"tensor": other},
        device_id_type=MESH,
    )
    base_copy.start()

    for copy in loads:
        copy.wait()
    scale = HEAD ** (-0.5)
    unroll = 4

    def old(i, carry):
        for u in range(unroll):
            r = i * unroll + u
            span = pl.ds(pl.multiple_of(r * per_row, per_row), per_row)
            query = qbuf[span, :]
            blank = jnp.zeros((per_group, HEAD), BF16)
            lhs = jnp.concatenate(
                [
                    jnp.concatenate(
                        [
                            query[g * per_group : (g + 1) * per_group] if g == k else blank
                            for k in range(groups)
                        ],
                        axis=1,
                    )
                    for g in range(groups)
                ],
                axis=0,
            )
            s = (
                lax.dot_general(
                    lhs, cbuf[r, 0], (((1,), (1,)), ((), ())), preferred_element_type=F32
                )
                * scale
            )
            s = jnp.where(iota(s.shape, 1) < len_ref[r], s, -1e30)
            m = jnp.max(s, axis=1, keepdims=True)
            e = jnp.exp(s - m)
            o = jnp.dot(e.astype(BF16), cbuf[r, 1], preferred_element_type=F32)
            top[span, :] = jnp.broadcast_to(m, (per_row, HEAD))
            total[span, :] = jnp.broadcast_to(
                jnp.sum(e, axis=1, keepdims=True), (per_row, HEAD)
            )
            mixed[span, :] = jnp.concatenate(
                [
                    o[g * per_group : (g + 1) * per_group, g * HEAD : (g + 1) * HEAD]
                    for g in range(groups)
                ],
                axis=0,
            )
        return carry

    lax.fori_loop(0, rows // unroll, old, 0)

    for copy in dispatch:
        copy.wait_recv()
    mid[...] = jnp.dot(recvbuf[...], dbuf[...], preferred_element_type=F32)
    mid_copy = pltpu.make_async_remote_copy(
        src_ref=mid,
        dst_ref=mid_in,
        send_sem=pair_send.at[1],
        recv_sem=pair_recv.at[1],
        device_id={"tensor": other},
        device_id_type=MESH,
    )
    mid_copy.start()
    up = up_ref[...]
    none = jnp.zeros(up.shape[1:], BF16)
    up_both = jnp.concatenate(
        [jnp.concatenate([up[0], none], axis=1), jnp.concatenate([none, up[1]], axis=1)], axis=0
    )
    mid_copy.wait_recv()
    middle = mid[...] + mid_in[...]
    high = middle.astype(BF16)
    low = (middle - high.astype(F32)).astype(BF16)
    ans[...] = (
        jnp.dot(high, up_both, preferred_element_type=F32)
        + jnp.dot(low, up_both, preferred_element_type=F32)
    ).astype(BF16)
    returns = []
    for o in order:
        d = lax.rem(me + o, n)
        returns.append(
            pltpu.make_async_remote_copy(
                src_ref=ans.at[block(d), :],
                dst_ref=ret.at[mine, :],
                send_sem=ret_send.at[o],
                recv_sem=ret_recv.at[o],
                device_id={"dp": d},
                device_id_type=MESH,
            )
        )
    for copy in returns:
        copy.start()
    ret[mine, :] = ans[mine, :]
    base_copy.wait_recv()
    for copy in returns:
        copy.wait_recv()
    delta = jnp.dot(back_t[...], ret[...], preferred_element_type=F32)
    own = half * 128
    packed = jnp.zeros((rows * 2 * groups, HEAD), F32)
    for j in range(2):
        part = slice(j * rows, (j + 1) * rows)
        value = base[side, part, :] + base_in[part, :] + delta[:, j * own : (j + 1) * own]
        value = value.astype(BF16)
        newkv[j] = value.astype(F32)
        for g in range(groups):
            shape = (rows * 2 * groups, rows)
            put = jnp.where(
                iota(shape, 0) == 2 * groups * iota(shape, 1) + 2 * g + j, 1.0, 0.0
            ).astype(BF16)
            packed = packed + jnp.dot(
                put, value[:, g * HEAD : (g + 1) * HEAD], preferred_element_type=F32
            )
    kv_ref[...] = packed.astype(BF16)

    many = 8

    def finish(i, carry):
        here = pl.ds(pl.multiple_of(i * many, many), many)
        keys = newkv[0, here, :]
        values = newkv[1, here, :]
        for u in range(many):
            r = i * many + u
            for g in range(groups):
                at = pl.multiple_of(r * per_row + g * per_group, per_group)
                span = pl.ds(at, per_group)
                key = keys[u : u + 1, g * HEAD : (g + 1) * HEAD]
                value = values[u : u + 1, g * HEAD : (g + 1) * HEAD]
                s = jnp.sum(qbuf[span, :].astype(F32) * key, axis=1, keepdims=True) * scale
                was = top[span, :]
                now = jnp.maximum(was, s)
                a = jnp.exp(was - now)
                b = jnp.exp(s - now)
                whole = total[span, :] * a + b
                out_ref[span, :] = ((mixed[span, :] * a + b * value) / whole).astype(BF16)
        return carry

    lax.fori_loop(0, rows // many, finish, 0)
    for copy in dispatch:
        copy.wait_send()
    for copy in returns:
        copy.wait_send()
    base_copy.wait_send()
    mid_copy.wait_send()


def per_device(hid, queries, cache, base_w, down_w, up_w, index, placement, lengths):
    n = lax.axis_size("dp")
    rows, width = hid.shape
    heads = queries.shape[2] // HEAD
    tiles = base_w.shape[2] // 128
    groups = cache.shape[3] // HEAD
    slots = n * SLOTS
    q = queries.reshape(rows, 2, heads, HEAD).transpose(0, 2, 1, 3).reshape(-1, HEAD)
    own = cache.shape[3]
    rank = down_w.shape[2]
    vmem = pl.BlockSpec(memory_space=pltpu.VMEM)
    smem = pl.BlockSpec(memory_space=pltpu.SMEM)
    hbm = pl.BlockSpec(memory_space=pl.ANY)
    out, kv = pl.pallas_call(
        functools.partial(kernel, n),
        out_shape=(
            jax.ShapeDtypeStruct(q.shape, BF16),
            jax.ShapeDtypeStruct((rows * 2 * groups, HEAD), BF16),
        ),
        in_specs=[vmem, vmem, smem, smem, vmem, hbm, hbm, hbm, hbm],
        out_specs=(vmem, vmem),
        scratch_shapes=[
            pltpu.VMEM(q.shape, BF16),
            pltpu.VMEM(cache.shape, BF16),
            pltpu.VMEM((tiles, width, 2, 128), BF16),
            pltpu.VMEM((width, rank), BF16),
            pltpu.VMEM((slots, width), BF16),
            pltpu.VMEM((slots, width), BF16),
            pltpu.VMEM((2 * rows, 2 * width), BF16),
            pltpu.VMEM((rows, slots), BF16),
            pltpu.VMEM((2, 2 * rows, own), F32),
            pltpu.VMEM((2 * rows, own), F32),
            pltpu.VMEM((slots, rank), F32),
            pltpu.VMEM((slots, rank), F32),
            pltpu.VMEM((slots, 2 * own), BF16),
            pltpu.VMEM((slots, 2 * own), BF16),
            pltpu.VMEM((2, rows, own), F32),
            pltpu.VMEM(q.shape, F32),
            pltpu.VMEM(q.shape, F32),
            pltpu.VMEM(q.shape, F32),
            pltpu.SemaphoreType.DMA((3,)),
            pltpu.SemaphoreType.DMA((tiles,)),
            pltpu.SemaphoreType.DMA((n,)),
            pltpu.SemaphoreType.DMA((n,)),
            pltpu.SemaphoreType.DMA((n,)),
            pltpu.SemaphoreType.DMA((n,)),
            pltpu.SemaphoreType.DMA((2,)),
            pltpu.SemaphoreType.DMA((2,)),
        ],
        compiler_params=pltpu.CompilerParams(
            collective_id=0, has_side_effects=True, vmem_limit_bytes=56 * 1024 * 1024
        ),
    )(
        hid,
        index.reshape(1, rows),
        placement,
        lengths,
        up_w[0],
        q,
        cache,
        base_w,
        down_w[0],
    )
    out = out.reshape(rows, heads, 2, HEAD).transpose(0, 2, 1, 3).reshape(rows, 2, -1)
    kv = kv.reshape(rows, groups, 2, HEAD).transpose(0, 2, 1, 3).reshape(rows, 2, -1)
    return out, kv


def solution(mesh):
    placed = (
        P(("rep", "dp"), "tensor"),
        P(("rep", "dp"), None, "tensor"),
        P(("rep", "dp"), None, None, "tensor"),
        P("tensor", None, None),
        P("dp", "tensor", None),
        P("dp", None, None, "tensor"),
        P(("rep", "dp"), None),
        P(),
        P(("rep", "dp")),
    )
    return jax.shard_map(
        per_device,
        mesh=mesh,
        in_specs=placed,
        out_specs=(P(("rep", "dp"), None, "tensor"), P(("rep", "dp"), None, "tensor")),
        check_vma=False,
    )
```

```python
import functools

import jax
import jax.numpy as jnp
from jax import lax
from jax.experimental import pallas as pl
from jax.experimental.pallas import tpu as pltpu
from jax.sharding import PartitionSpec as P

HEAD = 128
MESH = pl.DeviceIdType.MESH
BF16 = jnp.bfloat16
F32 = jnp.float32
SLOTS = 16


def iota(shape, dim):
    return lax.broadcasted_iota(jnp.int32, shape, dim)


def kernel(
    n,
    hid_ref,
    idx_ref,
    place_ref,
    len_ref,
    up_ref,
    q_hbm,
    cache_hbm,
    w_hbm,
    d_hbm,
    out_ref,
    kv_ref,
    qbuf,
    cbuf,
    wbuf,
    dbuf,
    sendbuf,
    recvbuf,
    wide,
    back_t,
    base,
    base_in,
    mid,
    mid_in,
    ans,
    ret,
    newkv,
    top,
    total,
    mixed,
    local_sem,
    w_sem,
    out_send,
    out_recv,
    ret_send,
    ret_recv,
    pair_send,
    pair_recv,
):
    rows, width = hid_ref.shape
    tiles = wbuf.shape[0]
    half = tiles // 2
    groups = cbuf.shape[3] // HEAD
    slots = n * SLOTS
    me = lax.axis_index("dp")
    side = lax.axis_index("tensor")
    other = 1 - side
    per_row = qbuf.shape[0] // rows
    per_group = per_row // groups

    loads = [
        pltpu.make_async_copy(q_hbm, qbuf, local_sem.at[0]),
        pltpu.make_async_copy(cache_hbm, cbuf, local_sem.at[1]),
        pltpu.make_async_copy(d_hbm, dbuf, local_sem.at[2]),
    ]
    w_loads = [
        pltpu.make_async_copy(w_hbm.at[:, :, pl.ds(c * 128, 128)], wbuf.at[c], w_sem.at[c])
        for c in range(tiles)
    ]

    barrier = pltpu.get_barrier_semaphore()
    for o in range(1, n):
        pl.semaphore_signal(
            barrier, inc=1, device_id={"dp": lax.rem(me + o, n)}, device_id_type=MESH
        )
    pl.semaphore_signal(barrier, inc=1, device_id={"tensor": other}, device_id_type=MESH)
    for copy in w_loads:
        copy.start()
    for copy in loads:
        copy.start()

    index = idx_ref[...]
    slot = jnp.zeros((1, rows), jnp.int32)
    for a in range(n):
        slot = slot + jnp.where(index == a, place_ref[a], 0)
    slot = slot.astype(F32)
    first, second = iota((rows, rows), 0), iota((rows, rows), 1)
    across = jnp.broadcast_to(slot, (rows, rows))
    down = jnp.sum(jnp.where(first == second, across, 0.0), axis=1, keepdims=True)
    same = jnp.where((down == across) & (first < second), 1.0, 0.0)
    target = slot * SLOTS + jnp.sum(same, axis=0, keepdims=True)
    target_down = jnp.sum(
        jnp.where(first == second, jnp.broadcast_to(target, (rows, rows)), 0.0),
        axis=1,
        keepdims=True,
    )
    placing = jnp.where(iota((slots, rows), 0).astype(F32) == target, 1.0, 0.0).astype(BF16)
    back_t[...] = jnp.where(
        iota((rows, slots), 1).astype(F32) == target_down, 1.0, 0.0
    ).astype(BF16)
    step = 1024
    for c in range(0, width, step):
        sendbuf[:, c : c + step] = jnp.dot(
            placing, hid_ref[:, c : c + step], preferred_element_type=F32
        ).astype(BF16)

    pl.semaphore_wait(barrier, n)
    mine = pl.ds(pl.multiple_of(me * SLOTS, SLOTS), SLOTS)

    def block(d):
        return pl.ds(pl.multiple_of(d * SLOTS, SLOTS), SLOTS)

    order = sorted(range(1, n), key=lambda o: -min(o, n - o))
    dispatch = []
    for o in order:
        d = lax.rem(me + o, n)
        dispatch.append(
            pltpu.make_async_remote_copy(
                src_ref=sendbuf.at[block(d), :],
                dst_ref=recvbuf.at[mine, :],
                send_sem=out_send.at[o],
                recv_sem=out_recv.at[o],
                device_id={"dp": d},
                device_id_type=MESH,
            )
        )
    for copy in dispatch:
        copy.start()
    recvbuf[mine, :] = sendbuf[mine, :]

    deep = 256
    spreads = [
        jnp.where(iota((deep, 2 * deep), 1) == 2 * iota((deep, 2 * deep), 0) + j, 1.0, 0.0).astype(
            BF16
        )
        for j in range(2)
    ]
    gang = 4
    for c in range(0, width, gang * deep):
        stack = jnp.concatenate(
            [hid_ref[:, c + i * deep : c + (i + 1) * deep] for i in range(gang)], axis=0
        )
        for j in range(2):
            res = jnp.dot(stack, spreads[j], preferred_element_type=F32).astype(BF16)
            for i in range(gang):
                at = 2 * (c + i * deep)
                wide[j * rows : (j + 1) * rows, at : at + 2 * deep] = res[
                    i * rows : (i + 1) * rows
                ]
    for copy in w_loads:
        copy.wait()
    chunk = 2048
    for h in range(2):
        acc = jnp.zeros((2 * rows, half * 128), F32)
        for k in range(0, 2 * width, chunk):
            rhs = jnp.concatenate(
                [
                    wbuf.at[h * half + c].reshape(2 * width, 128)[k : k + chunk, :]
                    for c in range(half)
                ],
                axis=1,
            )
            acc = acc + jnp.dot(wide[:, k : k + chunk], rhs, preferred_element_type=F32)
        base[h] = acc
    base_copy = pltpu.make_async_remote_copy(
        src_ref=base.at[other],
        dst_ref=base_in,
        send_sem=pair_send.at[0],
        recv_sem=pair_recv.at[0],
        device_id={"tensor": other},
        device_id_type=MESH,
    )
    base_copy.start()

    for copy in loads:
        copy.wait()
    scale = HEAD ** (-0.5)
    unroll = 8

    def spread(query):
        blank = jnp.zeros((per_group, HEAD), BF16)
        return jnp.concatenate(
            [
                jnp.concatenate(
                    [
                        query[g * per_group : (g + 1) * per_group] if g == k else blank
                        for k in range(groups)
                    ],
                    axis=1,
                )
                for g in range(groups)
            ],
            axis=0,
        )

    def old(i, carry):
        members = [i * unroll + u for u in range(unroll)]
        spans = [pl.ds(pl.multiple_of(r * per_row, per_row), per_row) for r in members]
        scores = [
            lax.dot_general(
                spread(qbuf[span, :]),
                cbuf[r, 0],
                (((1,), (1,)), ((), ())),
                preferred_element_type=F32,
            )
            for r, span in zip(members, spans)
        ]
        scores = [
            jnp.where(iota(s.shape, 1) < len_ref[r], s * scale, -1e30)
            for r, s in zip(members, scores)
        ]
        tops = [jnp.max(s, axis=1, keepdims=True) for s in scores]
        weights = [jnp.exp(s - m) for s, m in zip(scores, tops)]
        outs = [
            jnp.dot(e.astype(BF16), cbuf[r, 1], preferred_element_type=F32)
            for r, e in zip(members, weights)
        ]
        sums = [jnp.sum(e, axis=1, keepdims=True) for e in weights]
        for span, m, l, o in zip(spans, tops, sums, outs):
            top[span, :] = jnp.broadcast_to(m, (per_row, HEAD))
            total[span, :] = jnp.broadcast_to(l, (per_row, HEAD))
            for g in range(groups):
                part = slice(g * per_group, (g + 1) * per_group)
                at = pl.ds(pl.multiple_of(span.start + g * per_group, per_group), per_group)
                mixed[at, :] = o[part, g * HEAD : (g + 1) * HEAD]
        return carry

    lax.fori_loop(0, rows // unroll, old, 0)

    for copy in dispatch:
        copy.wait_recv()
    mid[...] = jnp.dot(recvbuf[...], dbuf[...], preferred_element_type=F32)
    mid_copy = pltpu.make_async_remote_copy(
        src_ref=mid,
        dst_ref=mid_in,
        send_sem=pair_send.at[1],
        recv_sem=pair_recv.at[1],
        device_id={"tensor": other},
        device_id_type=MESH,
    )
    mid_copy.start()
    up = up_ref[...]
    none = jnp.zeros(up.shape[1:], BF16)
    up_both = jnp.concatenate(
        [jnp.concatenate([up[0], none], axis=1), jnp.concatenate([none, up[1]], axis=1)], axis=0
    )
    mid_copy.wait_recv()
    middle = mid[...] + mid_in[...]
    high = middle.astype(BF16)
    low = (middle - high.astype(F32)).astype(BF16)
    ans[...] = (
        jnp.dot(high, up_both, preferred_element_type=F32)
        + jnp.dot(low, up_both, preferred_element_type=F32)
    ).astype(BF16)
    returns = []
    for o in order:
        d = lax.rem(me + o, n)
        returns.append(
            pltpu.make_async_remote_copy(
                src_ref=ans.at[block(d), :],
                dst_ref=ret.at[mine, :],
                send_sem=ret_send.at[o],
                recv_sem=ret_recv.at[o],
                device_id={"dp": d},
                device_id_type=MESH,
            )
        )
    for copy in returns:
        copy.start()
    ret[mine, :] = ans[mine, :]
    base_copy.wait_recv()
    for copy in returns:
        copy.wait_recv()
    delta = jnp.dot(back_t[...], ret[...], preferred_element_type=F32)
    own = half * 128
    packed = jnp.zeros((rows * 2 * groups, HEAD), F32)
    for j in range(2):
        part = slice(j * rows, (j + 1) * rows)
        value = base[side, part, :] + base_in[part, :] + delta[:, j * own : (j + 1) * own]
        value = value.astype(BF16)
        newkv[j] = value.astype(F32)
        for g in range(groups):
            shape = (rows * 2 * groups, rows)
            put = jnp.where(
                iota(shape, 0) == 2 * groups * iota(shape, 1) + 2 * g + j, 1.0, 0.0
            ).astype(BF16)
            packed = packed + jnp.dot(
                put, value[:, g * HEAD : (g + 1) * HEAD], preferred_element_type=F32
            )
    kv_ref[...] = packed.astype(BF16)

    many = 8

    def finish(i, carry):
        here = pl.ds(pl.multiple_of(i * many, many), many)
        keys = newkv[0, here, :]
        values = newkv[1, here, :]
        for u in range(many):
            r = i * many + u
            for g in range(groups):
                at = pl.multiple_of(r * per_row + g * per_group, per_group)
                span = pl.ds(at, per_group)
                key = keys[u : u + 1, g * HEAD : (g + 1) * HEAD]
                value = values[u : u + 1, g * HEAD : (g + 1) * HEAD]
                s = jnp.sum(qbuf[span, :].astype(F32) * key, axis=1, keepdims=True) * scale
                was = top[span, :]
                now = jnp.maximum(was, s)
                a = jnp.exp(was - now)
                b = jnp.exp(s - now)
                whole = total[span, :] * a + b
                out_ref[span, :] = ((mixed[span, :] * a + b * value) / whole).astype(BF16)
        return carry

    lax.fori_loop(0, rows // many, finish, 0)
    for copy in dispatch:
        copy.wait_send()
    for copy in returns:
        copy.wait_send()
    base_copy.wait_send()
    mid_copy.wait_send()


def land(a_ref, b_ref, x_ref, y_ref):
    x_ref[...] = a_ref[...]
    y_ref[...] = b_ref[...]


def per_device(hid, queries, cache, base_w, down_w, up_w, index, placement, lengths):
    n = lax.axis_size("dp")
    rows, width = hid.shape
    heads = queries.shape[2] // HEAD
    tiles = base_w.shape[2] // 128
    groups = cache.shape[3] // HEAD
    slots = n * SLOTS
    q = queries.reshape(rows, 2, heads, HEAD).transpose(0, 2, 1, 3).reshape(-1, HEAD)
    own = cache.shape[3]
    rank = down_w.shape[2]
    vmem = pl.BlockSpec(memory_space=pltpu.VMEM)
    smem = pl.BlockSpec(memory_space=pltpu.SMEM)
    hbm = pl.BlockSpec(memory_space=pl.ANY)
    out, kv = pl.pallas_call(
        functools.partial(kernel, n),
        out_shape=(
            jax.ShapeDtypeStruct(q.shape, BF16),
            jax.ShapeDtypeStruct((rows * 2 * groups, HEAD), BF16),
        ),
        in_specs=[vmem, vmem, smem, smem, vmem, hbm, hbm, hbm, hbm],
        out_specs=(vmem, vmem),
        scratch_shapes=[
            pltpu.VMEM(q.shape, BF16),
            pltpu.VMEM(cache.shape, BF16),
            pltpu.VMEM((tiles, width, 2, 128), BF16),
            pltpu.VMEM((width, rank), BF16),
            pltpu.VMEM((slots, width), BF16),
            pltpu.VMEM((slots, width), BF16),
            pltpu.VMEM((2 * rows, 2 * width), BF16),
            pltpu.VMEM((rows, slots), BF16),
            pltpu.VMEM((2, 2 * rows, own), F32),
            pltpu.VMEM((2 * rows, own), F32),
            pltpu.VMEM((slots, rank), F32),
            pltpu.VMEM((slots, rank), F32),
            pltpu.VMEM((slots, 2 * own), BF16),
            pltpu.VMEM((slots, 2 * own), BF16),
            pltpu.VMEM((2, rows, own), F32),
            pltpu.VMEM(q.shape, F32),
            pltpu.VMEM(q.shape, F32),
            pltpu.VMEM(q.shape, F32),
            pltpu.SemaphoreType.DMA((3,)),
            pltpu.SemaphoreType.DMA((tiles,)),
            pltpu.SemaphoreType.DMA((n,)),
            pltpu.SemaphoreType.DMA((n,)),
            pltpu.SemaphoreType.DMA((n,)),
            pltpu.SemaphoreType.DMA((n,)),
            pltpu.SemaphoreType.DMA((2,)),
            pltpu.SemaphoreType.DMA((2,)),
        ],
        compiler_params=pltpu.CompilerParams(
            collective_id=0, has_side_effects=True, vmem_limit_bytes=56 * 1024 * 1024
        ),
    )(
        hid,
        index.reshape(1, rows),
        placement,
        lengths,
        up_w[0],
        q,
        cache,
        base_w,
        down_w[0],
    )
    out, kv = pl.pallas_call(
        land,
        out_shape=(
            jax.ShapeDtypeStruct(out.shape, BF16),
            jax.ShapeDtypeStruct(kv.shape, BF16),
        ),
        in_specs=[vmem, vmem],
        out_specs=(vmem, vmem),
    )(out, kv)
    out = out.reshape(rows, heads, 2, HEAD).transpose(0, 2, 1, 3).reshape(rows, 2, -1)
    kv = kv.reshape(rows, groups, 2, HEAD).transpose(0, 2, 1, 3).reshape(rows, 2, -1)
    return out, kv


def solution(mesh):
    placed = (
        P(("rep", "dp"), "tensor"),
        P(("rep", "dp"), None, "tensor"),
        P(("rep", "dp"), None, None, "tensor"),
        P("tensor", None, None),
        P("dp", "tensor", None),
        P("dp", None, None, "tensor"),
        P(("rep", "dp"), None),
        P(),
        P(("rep", "dp")),
    )
    return jax.shard_map(
        per_device,
        mesh=mesh,
        in_specs=placed,
        out_specs=(P(("rep", "dp"), None, "tensor"), P(("rep", "dp"), None, "tensor")),
        check_vma=False,
    )
```

```python
import functools

import jax
import jax.numpy as jnp
from jax import lax
from jax.experimental import pallas as pl
from jax.experimental.pallas import tpu as pltpu
from jax.sharding import PartitionSpec as P

HEAD = 128
MESH = pl.DeviceIdType.MESH
BF16 = jnp.bfloat16
F32 = jnp.float32
SLOTS = 16


def iota(shape, dim):
    return lax.broadcasted_iota(jnp.int32, shape, dim)


def kernel(
    n,
    hid_ref,
    idx_ref,
    place_ref,
    len_ref,
    up_ref,
    q_hbm,
    cache_hbm,
    w_hbm,
    d_hbm,
    out_ref,
    kv_ref,
    qbuf,
    cbuf,
    wbuf,
    dbuf,
    sendbuf,
    recvbuf,
    wide,
    back_t,
    base,
    base_in,
    mid,
    mid_in,
    ans,
    ret,
    newkv,
    top,
    total,
    mixed,
    local_sem,
    w_sem,
    out_send,
    out_recv,
    ret_send,
    ret_recv,
    pair_send,
    pair_recv,
):
    rows, width = hid_ref.shape
    tiles = wbuf.shape[0]
    half = tiles // 2
    groups = cbuf.shape[3] // HEAD
    slots = n * SLOTS
    me = lax.axis_index("dp")
    side = lax.axis_index("tensor")
    other = 1 - side
    per_row = qbuf.shape[0] // rows
    per_group = per_row // groups

    loads = [
        pltpu.make_async_copy(q_hbm, qbuf, local_sem.at[0]),
        pltpu.make_async_copy(cache_hbm, cbuf, local_sem.at[1]),
        pltpu.make_async_copy(d_hbm, dbuf, local_sem.at[2]),
    ]
    w_loads = [
        pltpu.make_async_copy(w_hbm.at[:, :, pl.ds(c * 128, 128)], wbuf.at[c], w_sem.at[c])
        for c in range(tiles)
    ]

    barrier = pltpu.get_barrier_semaphore()
    for o in range(1, n):
        pl.semaphore_signal(
            barrier, inc=1, device_id={"dp": lax.rem(me + o, n)}, device_id_type=MESH
        )
    pl.semaphore_signal(barrier, inc=1, device_id={"tensor": other}, device_id_type=MESH)
    for copy in w_loads:
        copy.start()
    for copy in loads:
        copy.start()

    index = idx_ref[...]
    slot = jnp.zeros((1, rows), jnp.int32)
    for a in range(n):
        slot = slot + jnp.where(index == a, place_ref[a], 0)
    slot = slot.astype(F32)
    first, second = iota((rows, rows), 0), iota((rows, rows), 1)
    across = jnp.broadcast_to(slot, (rows, rows))
    down = jnp.sum(jnp.where(first == second, across, 0.0), axis=1, keepdims=True)
    same = jnp.where((down == across) & (first < second), 1.0, 0.0)
    target = slot * SLOTS + jnp.sum(same, axis=0, keepdims=True)
    target_down = jnp.sum(
        jnp.where(first == second, jnp.broadcast_to(target, (rows, rows)), 0.0),
        axis=1,
        keepdims=True,
    )
    placing = jnp.where(iota((slots, rows), 0).astype(F32) == target, 1.0, 0.0).astype(BF16)
    back_t[...] = jnp.where(
        iota((rows, slots), 1).astype(F32) == target_down, 1.0, 0.0
    ).astype(BF16)
    step = 1024
    for c in range(0, width, step):
        sendbuf[:, c : c + step] = jnp.dot(
            placing, hid_ref[:, c : c + step], preferred_element_type=F32
        ).astype(BF16)

    pl.semaphore_wait(barrier, n)
    mine = pl.ds(pl.multiple_of(me * SLOTS, SLOTS), SLOTS)

    def block(d):
        return pl.ds(pl.multiple_of(d * SLOTS, SLOTS), SLOTS)

    order = sorted(range(1, n), key=lambda o: -min(o, n - o))
    dispatch = []
    for o in order:
        d = lax.rem(me + o, n)
        dispatch.append(
            pltpu.make_async_remote_copy(
                src_ref=sendbuf.at[block(d), :],
                dst_ref=recvbuf.at[mine, :],
                send_sem=out_send.at[o],
                recv_sem=out_recv.at[o],
                device_id={"dp": d},
                device_id_type=MESH,
            )
        )
    for copy in dispatch:
        copy.start()
    recvbuf[mine, :] = sendbuf[mine, :]

    deep = 256
    spreads = [
        jnp.where(iota((deep, 2 * deep), 1) == 2 * iota((deep, 2 * deep), 0) + j, 1.0, 0.0).astype(
            BF16
        )
        for j in range(2)
    ]
    gang = 4
    for c in range(0, width, gang * deep):
        stack = jnp.concatenate(
            [hid_ref[:, c + i * deep : c + (i + 1) * deep] for i in range(gang)], axis=0
        )
        for j in range(2):
            res = jnp.dot(stack, spreads[j], preferred_element_type=F32).astype(BF16)
            for i in range(gang):
                at = 2 * (c + i * deep)
                wide[j * rows : (j + 1) * rows, at : at + 2 * deep] = res[
                    i * rows : (i + 1) * rows
                ]
    for copy in w_loads:
        copy.wait()
    chunk = 2048
    for h in range(2):
        acc = jnp.zeros((2 * rows, half * 128), F32)
        for k in range(0, 2 * width, chunk):
            rhs = jnp.concatenate(
                [
                    wbuf.at[h * half + c].reshape(2 * width, 128)[k : k + chunk, :]
                    for c in range(half)
                ],
                axis=1,
            )
            acc = acc + jnp.dot(wide[:, k : k + chunk], rhs, preferred_element_type=F32)
        base[h] = acc
    base_copy = pltpu.make_async_remote_copy(
        src_ref=base.at[other],
        dst_ref=base_in,
        send_sem=pair_send.at[0],
        recv_sem=pair_recv.at[0],
        device_id={"tensor": other},
        device_id_type=MESH,
    )
    base_copy.start()

    for copy in loads:
        copy.wait()
    scale = HEAD ** (-0.5)
    unroll = 8

    def spread(query):
        blank = jnp.zeros((per_group, HEAD), BF16)
        return jnp.concatenate(
            [
                jnp.concatenate(
                    [
                        query[g * per_group : (g + 1) * per_group] if g == k else blank
                        for k in range(groups)
                    ],
                    axis=1,
                )
                for g in range(groups)
            ],
            axis=0,
        )

    def old(i, carry):
        members = [i * unroll + u for u in range(unroll)]
        spans = [pl.ds(pl.multiple_of(r * per_row, per_row), per_row) for r in members]
        scores = [
            lax.dot_general(
                spread(qbuf[span, :]),
                cbuf[r, 0],
                (((1,), (1,)), ((), ())),
                preferred_element_type=F32,
            )
            for r, span in zip(members, spans)
        ]
        scores = [
            jnp.where(iota(s.shape, 1) < len_ref[r], s * scale, -1e30)
            for r, s in zip(members, scores)
        ]
        tops = [jnp.max(s, axis=1, keepdims=True) for s in scores]
        weights = [jnp.exp(s - m) for s, m in zip(scores, tops)]
        outs = [
            jnp.dot(e.astype(BF16), cbuf[r, 1], preferred_element_type=F32)
            for r, e in zip(members, weights)
        ]
        sums = [jnp.sum(e, axis=1, keepdims=True) for e in weights]
        for span, m, l, o in zip(spans, tops, sums, outs):
            top[span, :] = jnp.broadcast_to(m, (per_row, HEAD))
            total[span, :] = jnp.broadcast_to(l, (per_row, HEAD))
            for g in range(groups):
                part = slice(g * per_group, (g + 1) * per_group)
                at = pl.ds(pl.multiple_of(span.start + g * per_group, per_group), per_group)
                mixed[at, :] = o[part, g * HEAD : (g + 1) * HEAD]
        return carry

    lax.fori_loop(0, rows // unroll, old, 0)

    for copy in dispatch:
        copy.wait_recv()
    mid[...] = jnp.dot(recvbuf[...], dbuf[...], preferred_element_type=F32)
    mid_copy = pltpu.make_async_remote_copy(
        src_ref=mid,
        dst_ref=mid_in,
        send_sem=pair_send.at[1],
        recv_sem=pair_recv.at[1],
        device_id={"tensor": other},
        device_id_type=MESH,
    )
    mid_copy.start()
    up = up_ref[...]
    none = jnp.zeros(up.shape[1:], BF16)
    up_both = jnp.concatenate(
        [jnp.concatenate([up[0], none], axis=1), jnp.concatenate([none, up[1]], axis=1)], axis=0
    )
    mid_copy.wait_recv()
    middle = mid[...] + mid_in[...]
    high = middle.astype(BF16)
    low = (middle - high.astype(F32)).astype(BF16)
    ans[...] = (
        jnp.dot(high, up_both, preferred_element_type=F32)
        + jnp.dot(low, up_both, preferred_element_type=F32)
    ).astype(BF16)
    returns = []
    for o in order:
        d = lax.rem(me + o, n)
        returns.append(
            pltpu.make_async_remote_copy(
                src_ref=ans.at[block(d), :],
                dst_ref=ret.at[mine, :],
                send_sem=ret_send.at[o],
                recv_sem=ret_recv.at[o],
                device_id={"dp": d},
                device_id_type=MESH,
            )
        )
    for copy in returns:
        copy.start()
    ret[mine, :] = ans[mine, :]
    base_copy.wait_recv()
    for copy in returns:
        copy.wait_recv()
    delta = jnp.dot(back_t[...], ret[...], preferred_element_type=F32)
    own = half * 128
    packed = jnp.zeros((rows * 2 * groups, HEAD), F32)
    for j in range(2):
        part = slice(j * rows, (j + 1) * rows)
        value = base[side, part, :] + base_in[part, :] + delta[:, j * own : (j + 1) * own]
        value = value.astype(BF16)
        newkv[j] = value.astype(F32)
        for g in range(groups):
            shape = (rows * 2 * groups, rows)
            put = jnp.where(
                iota(shape, 0) == 2 * groups * iota(shape, 1) + 2 * g + j, 1.0, 0.0
            ).astype(BF16)
            packed = packed + jnp.dot(
                put, value[:, g * HEAD : (g + 1) * HEAD], preferred_element_type=F32
            )
    kv_ref[...] = packed.astype(BF16)

    many = 8

    def finish(i, carry):
        here = pl.ds(pl.multiple_of(i * many, many), many)
        keys = newkv[0, here, :]
        values = newkv[1, here, :]
        pairs = [(u, g) for u in range(many) for g in range(groups)]
        spans = [
            pl.ds(
                pl.multiple_of((i * many + u) * per_row + g * per_group, per_group), per_group
            )
            for u, g in pairs
        ]
        keys = [keys[u : u + 1, g * HEAD : (g + 1) * HEAD] for u, g in pairs]
        values = [values[u : u + 1, g * HEAD : (g + 1) * HEAD] for u, g in pairs]
        scores = [
            jnp.sum(qbuf[span, :].astype(F32) * key, axis=1, keepdims=True) * scale
            for span, key in zip(spans, keys)
        ]
        results = []
        for span, s, value in zip(spans, scores, values):
            was = top[span, :]
            now = jnp.maximum(was, s)
            a = jnp.exp(was - now)
            b = jnp.exp(s - now)
            whole = total[span, :] * a + b
            results.append(((mixed[span, :] * a + b * value) / whole).astype(BF16))
        for span, result in zip(spans, results):
            out_ref[span, :] = result
        return carry

    lax.fori_loop(0, rows // many, finish, 0)
    for copy in dispatch:
        copy.wait_send()
    for copy in returns:
        copy.wait_send()
    base_copy.wait_send()
    mid_copy.wait_send()


def land(a_ref, b_ref, x_ref, y_ref):
    x_ref[...] = a_ref[...]
    y_ref[...] = b_ref[...]


def per_device(hid, queries, cache, base_w, down_w, up_w, index, placement, lengths):
    n = lax.axis_size("dp")
    rows, width = hid.shape
    heads = queries.shape[2] // HEAD
    tiles = base_w.shape[2] // 128
    groups = cache.shape[3] // HEAD
    slots = n * SLOTS
    q = queries.reshape(rows, 2, heads, HEAD).transpose(0, 2, 1, 3).reshape(-1, HEAD)
    own = cache.shape[3]
    rank = down_w.shape[2]
    vmem = pl.BlockSpec(memory_space=pltpu.VMEM)
    smem = pl.BlockSpec(memory_space=pltpu.SMEM)
    hbm = pl.BlockSpec(memory_space=pl.ANY)
    out, kv = pl.pallas_call(
        functools.partial(kernel, n),
        out_shape=(
            jax.ShapeDtypeStruct(q.shape, BF16),
            jax.ShapeDtypeStruct((rows * 2 * groups, HEAD), BF16),
        ),
        in_specs=[vmem, vmem, smem, smem, vmem, hbm, hbm, hbm, hbm],
        out_specs=(vmem, vmem),
        scratch_shapes=[
            pltpu.VMEM(q.shape, BF16),
            pltpu.VMEM(cache.shape, BF16),
            pltpu.VMEM((tiles, width, 2, 128), BF16),
            pltpu.VMEM((width, rank), BF16),
            pltpu.VMEM((slots, width), BF16),
            pltpu.VMEM((slots, width), BF16),
            pltpu.VMEM((2 * rows, 2 * width), BF16),
            pltpu.VMEM((rows, slots), BF16),
            pltpu.VMEM((2, 2 * rows, own), F32),
            pltpu.VMEM((2 * rows, own), F32),
            pltpu.VMEM((slots, rank), F32),
            pltpu.VMEM((slots, rank), F32),
            pltpu.VMEM((slots, 2 * own), BF16),
            pltpu.VMEM((slots, 2 * own), BF16),
            pltpu.VMEM((2, rows, own), F32),
            pltpu.VMEM(q.shape, F32),
            pltpu.VMEM(q.shape, F32),
            pltpu.VMEM(q.shape, F32),
            pltpu.SemaphoreType.DMA((3,)),
            pltpu.SemaphoreType.DMA((tiles,)),
            pltpu.SemaphoreType.DMA((n,)),
            pltpu.SemaphoreType.DMA((n,)),
            pltpu.SemaphoreType.DMA((n,)),
            pltpu.SemaphoreType.DMA((n,)),
            pltpu.SemaphoreType.DMA((2,)),
            pltpu.SemaphoreType.DMA((2,)),
        ],
        compiler_params=pltpu.CompilerParams(
            collective_id=0, has_side_effects=True, vmem_limit_bytes=56 * 1024 * 1024
        ),
    )(
        hid,
        index.reshape(1, rows),
        placement,
        lengths,
        up_w[0],
        q,
        cache,
        base_w,
        down_w[0],
    )
    out, kv = pl.pallas_call(
        land,
        out_shape=(
            jax.ShapeDtypeStruct(out.shape, BF16),
            jax.ShapeDtypeStruct(kv.shape, BF16),
        ),
        in_specs=[vmem, vmem],
        out_specs=(vmem, vmem),
    )(out, kv)
    out = out.reshape(rows, heads, 2, HEAD).transpose(0, 2, 1, 3).reshape(rows, 2, -1)
    kv = kv.reshape(rows, groups, 2, HEAD).transpose(0, 2, 1, 3).reshape(rows, 2, -1)
    return out, kv


def solution(mesh):
    placed = (
        P(("rep", "dp"), "tensor"),
        P(("rep", "dp"), None, "tensor"),
        P(("rep", "dp"), None, None, "tensor"),
        P("tensor", None, None),
        P("dp", "tensor", None),
        P("dp", None, None, "tensor"),
        P(("rep", "dp"), None),
        P(),
        P(("rep", "dp")),
    )
    return jax.shard_map(
        per_device,
        mesh=mesh,
        in_specs=placed,
        out_specs=(P(("rep", "dp"), None, "tensor"), P(("rep", "dp"), None, "tensor")),
        check_vma=False,
    )
```
